32 devices in a mesh: day: 16 (over z, y, x), space: 2 (over core).
Axes of the slice: x: 2, y: 2, z: 4, core: 2. Of those that a mesh axis runs over, the one named last changes fastest.
Arguments:
- latent_start: float32 [16, 6144], P('day', 'space'), may hold values from -3 to 3
- counts: int32 [16, 6144], P('day', 'space'), may hold values from 0 to 24
- log_exposure: float32 [16, 6144], P('day', 'space'), may hold values from -2.5 to 2.5
- time_rate: float32 [6144], P('space'), may hold values from 0.5 to 8
- diag_blocks: float32 [48, 128, 128], P('space'), may hold values from -0.008 to 6, as said below
- upper_blocks: float32 [48, 128, 128], P('space'), may hold values from -0.004 to 0.004
- columns: int32 [48], P('space'), may hold values from 0 to 47, as said below
- inverse_panels: float32 [48, 128, 128], P('space'), may hold values from -0.001 to 0.4, as said below
Outputs:
- latent: float32 [16, 6144], P('day', 'space')
- gradient: float32 [16, 6144], P('day', 'space')
The draws below stay inside these ranges and needn't reach their ends.
Inputs may be any that keep to these rules, and one draw needn't show every extreme that they name: Block row r's off-diagonal block column lies in the next aligned group of 24 block rows (for the last group, in that group itself), and the rows of one group name distinct columns. `diag_blocks`: Symmetric; each row's diagonal entry exceeds the sum of magnitudes of its other entries by 1.9 or more. `inverse_panels`: Symmetric; each row's diagonal entry exceeds the sum of magnitudes of its other entries.
All inputs are finite; a program needn't handle non-finite values.
Results may differ from the reference program's by a relative error of at most 0.0003.
Values sent between devices are 32-bit elements; how exact they have to be, the bound alone decides.
A program may use at most 64 MiB of HBM per device.

```python
import math
import jax
import jax.numpy as jnp
from jax import lax

BLOCK = 128
NB_DEV = 24
NEWTON = 2
ITERS = 3
NB = 48
NODES = 6144
DAYS = 16


def symmetric_part(key, bound):
    raw = jax.random.uniform(key, (NB, BLOCK, BLOCK), jnp.float32, -bound, bound)
    return 0.5 * (raw + jnp.swapaxes(raw, 1, 2))


def draw_diag_blocks(key, part):
    key = jax.random.fold_in(key, 11)
    key_diag, key_off = jax.random.split(key)
    diagonal = jax.random.uniform(key_diag, (NB, BLOCK), jnp.float32, 3.0, 6.0)
    identity = jnp.eye(BLOCK, dtype=jnp.float32)
    return symmetric_part(key_off, 0.008) * (1.0 - identity) + diagonal[:, :, None] * identity


def draw_upper_blocks(key, part):
    key = jax.random.fold_in(key, 23)
    key_own = jax.random.fold_in(key, 1)
    return jax.random.uniform(key_own, (NB, BLOCK, BLOCK), jnp.float32, -0.004, 0.004)


def draw_inverse_panels(key, part):
    key = jax.random.fold_in(key, 37)
    key_diag, key_off = jax.random.split(key)
    diagonal = jax.random.uniform(key_diag, (NB, BLOCK), jnp.float32, 0.15, 0.4)
    identity = jnp.eye(BLOCK, dtype=jnp.float32)
    return symmetric_part(key_off, 0.001) * (1.0 - identity) + diagonal[:, :, None] * identity


def draw_columns(key, part):
    key = jax.random.fold_in(key, 41)
    groups = NB // NB_DEV
    group_keys = jax.random.split(key, groups)
    perms = jax.vmap(lambda one_key: jax.random.permutation(one_key, NB_DEV))(group_keys)
    target = jnp.minimum(jnp.arange(groups) + 1, groups - 1)
    return (target[:, None] * NB_DEV + perms).reshape(NB).astype(jnp.int32)


def with_ends(drawn, rng, low, high):
    place = [jax.random.randint(jax.random.fold_in(rng, axis), (), 0, length) for axis, length in enumerate(drawn.shape)]
    longest = drawn.shape.index(max(drawn.shape))
    neighbour = place[:longest] + [(place[longest] + 1) % drawn.shape[longest]] + place[longest + 1:]
    return drawn.at[tuple(place)].set(low).at[tuple(neighbour)].set(high)


def block_scale(rng, shape, pieces, least, high):
    factor_of, own = 1.0, jax.random.fold_in(rng, 6)
    for position, blocks in pieces:
        draws = jnp.exp(jax.random.uniform(jax.random.fold_in(own, position), (blocks,), jnp.float32, least / len(pieces), high / len(pieces)))
        factor_of = factor_of * jnp.repeat(draws, shape[position] // blocks).reshape([-1 if axis == position else 1 for axis in range(len(shape))])
    return factor_of


def gaussian(key, shape, scale, most, pieces=(), held_as=jnp.bfloat16):
    values = jax.random.normal(key, shape, jnp.float32) * scale
    if len(pieces) > 0:
        values = block_scale(key, shape, pieces, -0.22, 0.18) * values
    return jnp.clip(values, min=-most, max=most).astype(held_as)


def setup_inputs(seed: int = 0) -> dict:
    key_of = jax.random.split(jax.random.key(seed), 9)
    latent_start = gaussian(key_of[0], (DAYS, NODES), 0.5, 3.0, ((0, 16), (1, 2)), jnp.float32)
    counts = with_ends(jax.random.randint(key_of[1], (DAYS, NODES), 0, 25), jax.random.fold_in(key_of[1], 1), 0, 24).astype(jnp.int32)
    log_exposure = gaussian(key_of[2], (DAYS, NODES), 0.5, 2.5, ((0, 16), (1, 2)), jnp.float32)
    time_rate = jnp.clip(jnp.exp(math.log(8.0) - 2.7725887 * jax.random.uniform(key_of[3], (NODES,), jnp.float32) ** block_scale(key_of[3], (NODES,), ((0, 2),), -0.2, 0.2)), 0.5, 8.0)
    diag_blocks = draw_diag_blocks(jax.random.fold_in(key_of[8], 71), 0)
    upper_blocks = draw_upper_blocks(jax.random.fold_in(key_of[8], 71), 0)
    columns = draw_columns(jax.random.fold_in(key_of[8], 71), 0)
    inverse_panels = draw_inverse_panels(jax.random.fold_in(key_of[8], 71), 0)
    return dict(latent_start=latent_start, counts=counts, log_exposure=log_exposure, time_rate=time_rate, diag_blocks=diag_blocks, upper_blocks=upper_blocks, columns=columns, inverse_panels=inverse_panels)


def spatial_apply(vector, diag_blocks, upper_blocks, columns):
    highest = lax.Precision.HIGHEST
    blocks = vector.reshape(DAYS, NB, BLOCK)
    own_part = jnp.einsum('bij,dbj->dbi', diag_blocks, blocks, precision=highest)
    ahead_part = jnp.einsum('bij,dbj->dbi', upper_blocks, blocks[:, columns], precision=highest)
    back_terms = jnp.einsum('bij,dbi->dbj', upper_blocks, blocks, precision=highest)
    behind = jnp.zeros_like(blocks).at[:, columns].add(back_terms)
    return (own_part + ahead_part + behind).reshape(DAYS, NODES)


def prior_apply(vector, time_rate, diag_blocks, upper_blocks, columns):
    padded = jnp.pad(vector, ((1, 1), (0, 0)))
    day_index = jnp.arange(DAYS)
    degree = 2.0 - jnp.where(day_index == 0, 1.0, 0.0) - jnp.where(day_index == DAYS - 1, 1.0, 0.0)
    temporal = time_rate[None, :] * (degree[:, None].astype(jnp.float32) * vector - padded[:-2] - padded[2:])
    return spatial_apply(vector, diag_blocks, upper_blocks, columns) + temporal


def precondition(residual, inverse_panels):
    blocks = residual.reshape(DAYS, NB, BLOCK)
    smoothed = jnp.einsum('bij,dbj->dbi', inverse_panels, blocks, precision=lax.Precision.HIGHEST)
    return smoothed.reshape(DAYS, NODES)


def reference(latent_start, counts, log_exposure, time_rate, diag_blocks, upper_blocks, columns, inverse_panels):
    observed = counts.astype(jnp.float32)
    latent = latent_start

    def prior(vector):
        return prior_apply(vector, time_rate, diag_blocks, upper_blocks, columns)

    for newton_step in range(NEWTON):
        weight = jnp.exp(latent + log_exposure)
        right_side = -(prior(latent) + weight - observed)
        update = jnp.zeros_like(latent)
        residual = right_side
        smoothed = precondition(residual, inverse_panels)
        direction = smoothed
        rz_now = jnp.sum(residual * smoothed)
        for inner in range(ITERS):
            image = prior(direction) + weight * direction
            step_size = rz_now / jnp.sum(direction * image)
            update = update + step_size * direction
            residual = residual - step_size * image
            if inner < ITERS - 1:
                smoothed = precondition(residual, inverse_panels)
                rz_next = jnp.sum(residual * smoothed)
                direction = smoothed + (rz_next / rz_now) * direction
                rz_now = rz_next
        latent = latent + update
    gradient = prior(latent) + jnp.exp(latent + log_exposure) - observed
    return latent, gradient
```

```python
import functools

import jax
import jax.numpy as jnp
from jax import lax
from jax.experimental import pallas as pl
from jax.experimental.pallas import tpu as pltpu
from jax.sharding import PartitionSpec as P

BLOCK = 128
NEWTON = 2
ITERS = 3
UNROLL = 4
MESH = pl.DeviceIdType.MESH


def split(value):
    high = value.astype(jnp.bfloat16)
    low = (value - high.astype(jnp.float32)).astype(jnp.bfloat16)
    return high, low


def product(value, weights):
    rows = value.shape[0]
    high, low = split(value)
    left = jnp.concatenate(
        [jnp.concatenate([high, high], axis=1), jnp.concatenate([low, low], axis=1)], axis=0
    )
    out = jnp.dot(left, weights, preferred_element_type=jnp.float32)
    return out[:rows] + out[rows:]


def kernel(
    days,
    spaces,
    group,
    latent_ref,
    counts_ref,
    exposure_ref,
    rate_ref,
    diag_ref,
    upper_ref,
    column_ref,
    inverse_ref,
    panel_ref,
    latent_out,
    gradient_out,
    gath,
    lat,
    expo,
    weight,
    resid,
    smooth,
    direc,
    image,
    dimage,
    update,
    back_tmp,
    back_send,
    field_first,
    field_later,
    back_recv,
    red,
    w_du,
    w_ut,
    w_m,
    gs_sem,
    gr_sem,
    fs_sem,
    fr_sem,
    bs_sem,
    br_sem,
    rs_sem,
    rr_sem,
):
    day = lax.axis_index("day")
    me = lax.axis_index("space")
    last = spaces - 1
    stages = days.bit_length() - 1

    def reverse(index):
        out = index * 0
        for bit in range(stages):
            out = out + ((index // (1 << bit)) % 2) * (days >> (bit + 1))
        return out

    def partner(stage):
        step = days >> (stage + 1)
        return day + step - 2 * step * ((day // step) % 2)

    barrier = pltpu.get_barrier_semaphore()
    for stage in range(stages):
        pl.semaphore_signal(barrier, inc=1, device_id=(partner(stage), me), device_id_type=MESH)
    for offset in range(1, spaces):
        pl.semaphore_signal(
            barrier, inc=1, device_id=(day, lax.rem(me + offset, spaces)), device_id_type=MESH
        )

    place = reverse(day)
    gath[place, 0] = latent_ref[...]
    gath[place, 1] = latent_ref[...] + exposure_ref[...]
    gath[place, 2] = counts_ref[...].astype(jnp.float32)

    pl.semaphore_wait(barrier, stages + spaces - 1)

    def prepare(b):
        high, low = split(diag_ref[b])
        w_du[b, :BLOCK, :BLOCK] = high
        w_du[b, BLOCK:, :BLOCK] = low
        upper = upper_ref[b]
        high, low = split(upper)
        w_du[b, :BLOCK, BLOCK:] = high
        w_du[b, BLOCK:, BLOCK:] = low
        high, low = split(upper.T)
        w_ut[b, :BLOCK] = high
        w_ut[b, BLOCK:] = low
        high, low = split(panel_ref[b])
        w_m[b, :BLOCK] = high
        w_m[b, BLOCK:] = low

    for stage in range(stages):
        rows = 1 << stage
        base = (place // rows) * rows
        held = gath.at[pl.ds(base, rows)]
        copy = pltpu.make_async_remote_copy(
            src_ref=held,
            dst_ref=held,
            send_sem=gs_sem.at[stage],
            recv_sem=gr_sem.at[stage],
            device_id=(partner(stage), me),
            device_id_type=MESH,
        )
        copy.start()
        low, high = group * stage // stages, group * (stage + 1) // stages

        @pl.loop(low, high)
        def _(b):
            prepare(b)

        copy.wait()

    for d in range(days):
        spot = int(format(d, "0%db" % stages)[::-1], 2)
        smooth[:, d, :] = gath[spot, 0]
        expo[:, d, :] = gath[spot, 1]
        resid[:, d, :] = gath[spot, 2]

    def each(body):
        @pl.loop(0, group // UNROLL)
        def _(step):
            for i in range(UNROLL):
                body(step * UNROLL + i)

    rows = lax.broadcasted_iota(jnp.int32, (days, BLOCK), 0)
    first_day, last_day = rows == 0, rows == days - 1
    degree = 2.0 - jnp.where(first_day, 1.0, 0.0) - jnp.where(last_day, 1.0, 0.0)

    def prior(slot):
        field_recv = (field_first, field_later)[slot]
        field = pltpu.make_async_remote_copy(
            src_ref=smooth,
            dst_ref=field_recv,
            send_sem=fs_sem.at[slot],
            recv_sem=fr_sem.at[slot],
            device_id=(day, lax.rem(me + last, spaces)),
            device_id_type=MESH,
        )
        back = pltpu.make_async_remote_copy(
            src_ref=back_send,
            dst_ref=back_recv.at[slot],
            send_sem=bs_sem.at[slot],
            recv_sem=br_sem.at[slot],
            device_id=(day, lax.rem(me + 1, spaces)),
            device_id_type=MESH,
        )

        @pl.when(me > 0)
        def _():
            field.start()

        @pl.when(me == last)
        def _():
            field_recv[...] = smooth[...]

        def own(b):
            value = smooth[b]
            both = product(value, w_du[b])
            before = jnp.where(first_day, 0.0, pltpu.roll(value, 1, 0))
            after = jnp.where(last_day, 0.0, pltpu.roll(value, days - 1, 0))
            image[b] = both[:, :BLOCK] + rate_ref[b] * (degree * value - before - after)
            back_tmp[b] = both[:, BLOCK:]

        each(own)

        def permute(b):
            back_send[b] = back_tmp[inverse_ref[b]]

        each(permute)

        @pl.when(me < last)
        def _():
            back.start()
            field.wait_recv()

        def ahead(b):
            image[b] += product(field_recv[column_ref[b]], w_ut[b])

        each(ahead)

        @pl.when(me > 0)
        def _():
            back.wait_recv()
            image[...] += back_recv[slot]
            field.wait_send()

        @pl.when(me == last)
        def _():
            image[...] += back_send[...]

        @pl.when(me < last)
        def _():
            back.wait_send()

    prior(0)
    lat[...] = smooth[...]
    weight[...] = jnp.exp(expo[...])
    resid[...] = resid[...] - weight[...] - image[...]

    def reduced(slot, parts):
        red[slot, me] = jnp.concatenate(
            parts + [jnp.zeros((8 - len(parts), BLOCK), jnp.float32)], axis=0
        )
        copies = []
        for offset in range(1, spaces):
            mine = red.at[slot, me]
            copies.append(
                pltpu.make_async_remote_copy(
                    src_ref=mine,
                    dst_ref=mine,
                    send_sem=rs_sem.at[slot, offset],
                    recv_sem=rr_sem.at[slot, offset],
                    device_id=(day, lax.rem(me + offset, spaces)),
                    device_id_type=MESH,
                )
            )
        for copy in copies:
            copy.start()
        for copy in copies:
            copy.wait()
        total = red[slot, 0]
        for other in range(1, spaces):
            total = total + red[slot, other]
        sums = jnp.sum(total, axis=1, keepdims=True)
        return [sums[i : i + 1] for i in range(len(parts))]

    def across(value):
        return jnp.sum(jnp.sum(value, axis=0), axis=0, keepdims=True)

    one = jnp.ones((1, 1), jnp.float32)

    @pl.loop(0, NEWTON)
    def _(newton):
        direc[...] = jnp.zeros_like(direc)
        dimage[...] = jnp.zeros_like(dimage)
        update[...] = jnp.zeros_like(update)

        def iterate(inner, carry):
            rz_old, curve_old = carry
            count = newton * ITERS + inner

            def precondition(b):
                smooth[b] = product(resid[b], w_m[b])

            each(precondition)
            prior(1)
            image[...] += weight[...] * smooth[...]
            rz, straight, cross = reduced(
                lax.rem(count, 2),
                [
                    across(resid[...] * smooth[...]),
                    across(smooth[...] * image[...]),
                    across(smooth[...] * dimage[...]),
                ],
            )
            ratio = jnp.where(inner == 0, 0.0, rz / rz_old)
            curve = straight + 2.0 * ratio * cross + ratio * ratio * curve_old
            size = rz / curve
            direc[...] = smooth[...] + ratio * direc[...]
            dimage[...] = image[...] + ratio * dimage[...]
            update[...] += size * direc[...]
            resid[...] -= size * dimage[...]
            return rz, curve

        lax.fori_loop(0, ITERS, iterate, (one, one))
        lat[...] += update[...]
        expo[...] += update[...]
        fresh = jnp.exp(expo[...])
        resid[...] = resid[...] + weight[...] * (1.0 + update[...]) - fresh
        weight[...] = fresh

    mine = lax.broadcasted_iota(jnp.int32, (group, days, BLOCK), 1) == day
    latent_out[...] = jnp.sum(jnp.where(mine, lat[...], 0.0), axis=1)
    gradient_out[...] = -jnp.sum(jnp.where(mine, resid[...], 0.0), axis=1)


def on_device(
    latent_start,
    counts,
    log_exposure,
    time_rate,
    diag_blocks,
    upper_blocks,
    columns,
    inverse_panels,
):
    local_days, width = latent_start.shape
    group = diag_blocks.shape[0]
    spaces = lax.axis_size("space")
    days = local_days * lax.axis_size("day")
    stages = days.bit_length() - 1
    local = columns % group
    match = local[:, None] == jnp.arange(group)[None, :]
    inverse = jnp.sum(jnp.where(match, jnp.arange(group)[:, None], 0), axis=0).astype(jnp.int32)
    field = (group, days, BLOCK)
    vmem = pl.BlockSpec(memory_space=pltpu.VMEM)
    smem = pl.BlockSpec(memory_space=pltpu.SMEM)
    sem = pltpu.SemaphoreType.DMA
    f32, bf16 = jnp.float32, jnp.bfloat16
    shape = (group, BLOCK)
    latent, gradient = pl.pallas_call(
        functools.partial(kernel, days, spaces, group),
        out_shape=[jax.ShapeDtypeStruct(shape, f32)] * 2,
        in_specs=[vmem] * 6 + [smem] * 2 + [vmem],
        out_specs=[vmem] * 2,
        scratch_shapes=[pltpu.VMEM((days, 3) + shape, f32)]
        + [pltpu.VMEM(field, f32)] * 13
        + [pltpu.VMEM((2,) + field, f32)]
        + [
            pltpu.VMEM((2, spaces, 8, BLOCK), f32),
            pltpu.VMEM((group, 2 * BLOCK, 2 * BLOCK), bf16),
            pltpu.VMEM((group, 2 * BLOCK, BLOCK), bf16),
            pltpu.VMEM((group, 2 * BLOCK, BLOCK), bf16),
            sem((stages,)),
            sem((stages,)),
            sem((2,)),
            sem((2,)),
            sem((2,)),
            sem((2,)),
            sem((2, spaces)),
            sem((2, spaces)),
        ],
        compiler_params=pltpu.CompilerParams(
            collective_id=0, has_side_effects=True, vmem_limit_bytes=48 * 1024 * 1024
        ),
    )(
        latent_start.reshape(shape),
        counts.reshape(shape),
        log_exposure.reshape(shape),
        time_rate.reshape(group, 1, BLOCK),
        diag_blocks,
        upper_blocks,
        local,
        inverse,
        inverse_panels,
    )
    return latent.reshape(1, width), gradient.reshape(1, width)


def solution(mesh):
    placed = (
        P("day", "space"),
        P("day", "space"),
        P("day", "space"),
        P("space"),
        P("space", None, None),
        P("space", None, None),
        P("space"),
        P("space", None, None),
    )
    return jax.shard_map(
        on_device,
        mesh=mesh,
        in_specs=placed,
        out_specs=(P("day", "space"), P("day", "space")),
        check_vma=False,
    )
```

```python
import functools

import jax
import jax.numpy as jnp
from jax import lax
from jax.experimental import pallas as pl
from jax.experimental.pallas import tpu as pltpu
from jax.sharding import PartitionSpec as P

BLOCK = 128
NEWTON = 2
ITERS = 3
UNROLL = 4
MESH = pl.DeviceIdType.MESH


def split(value):
    high = value.astype(jnp.bfloat16)
    low = (value - high.astype(jnp.float32)).astype(jnp.bfloat16)
    return high, low


def product(value, weights):
    rows = value.shape[0]
    high, low = split(value)
    left = jnp.concatenate(
        [jnp.concatenate([high, high], axis=1), jnp.concatenate([low, low], axis=1)], axis=0
    )
    out = jnp.dot(left, weights, preferred_element_type=jnp.float32)
    return out[:rows] + out[rows:]


def kernel(
    days,
    spaces,
    group,
    latent_hbm,
    counts_hbm,
    exposure_hbm,
    rate_hbm,
    diag_hbm,
    upper_hbm,
    column_ref,
    inverse_ref,
    panel_hbm,
    latent_out,
    gradient_out,
    latent_ref,
    counts_ref,
    exposure_ref,
    rate_ref,
    diag_ref,
    upper_ref,
    panel_ref,
    in_sem,
    gath,
    lat,
    expo,
    weight,
    resid,
    smooth,
    direc,
    image,
    dimage,
    update,
    back_tmp,
    back_send,
    field_first,
    field_later,
    back_recv,
    red,
    w_du,
    w_ut,
    w_m,
    gs_sem,
    gr_sem,
    fs_sem,
    fr_sem,
    bs_sem,
    br_sem,
    rs_sem,
    rr_sem,
):
    day = lax.axis_index("day")
    me = lax.axis_index("space")
    last = spaces - 1
    stages = days.bit_length() - 1

    def reverse(index):
        out = index * 0
        for bit in range(stages):
            out = out + ((index // (1 << bit)) % 2) * (days >> (bit + 1))
        return out

    def partner(stage):
        step = days >> (stage + 1)
        return day + step - 2 * step * ((day // step) % 2)

    sources = (latent_hbm, exposure_hbm, counts_hbm, rate_hbm, diag_hbm, upper_hbm, panel_hbm)
    targets = (latent_ref, exposure_ref, counts_ref, rate_ref, diag_ref, upper_ref, panel_ref)
    loads = [
        pltpu.make_async_copy(source, target, in_sem.at[i])
        for i, (source, target) in enumerate(zip(sources, targets))
    ]
    for load in loads:
        load.start()

    barrier = pltpu.get_barrier_semaphore()
    for stage in range(stages):
        pl.semaphore_signal(barrier, inc=1, device_id=(partner(stage), me), device_id_type=MESH)
    for offset in range(1, spaces):
        pl.semaphore_signal(
            barrier, inc=1, device_id=(day, lax.rem(me + offset, spaces)), device_id_type=MESH
        )

    place = reverse(day)
    for load in loads[:3]:
        load.wait()
    gath[place, 0] = latent_ref[...]
    gath[place, 1] = latent_ref[...] + exposure_ref[...]
    gath[place, 2] = counts_ref[...].astype(jnp.float32)

    pl.semaphore_wait(barrier, stages + spaces - 1)

    def prepare(b):
        high, low = split(diag_ref[b])
        w_du[b, :BLOCK, :BLOCK] = high
        w_du[b, BLOCK:, :BLOCK] = low
        upper = upper_ref[b]
        high, low = split(upper)
        w_du[b, :BLOCK, BLOCK:] = high
        w_du[b, BLOCK:, BLOCK:] = low
        high, low = split(upper.T)
        w_ut[b, :BLOCK] = high
        w_ut[b, BLOCK:] = low
        high, low = split(panel_ref[b])
        w_m[b, :BLOCK] = high
        w_m[b, BLOCK:] = low

    for stage in range(stages):
        rows = 1 << stage
        base = (place // rows) * rows
        held = gath.at[pl.ds(base, rows)]
        copy = pltpu.make_async_remote_copy(
            src_ref=held,
            dst_ref=held,
            send_sem=gs_sem.at[stage],
            recv_sem=gr_sem.at[stage],
            device_id=(partner(stage), me),
            device_id_type=MESH,
        )
        copy.start()
        if stage == 0:
            for load in loads[3:]:
                load.wait()
        low, high = group * stage // stages, group * (stage + 1) // stages

        @pl.loop(low, high)
        def _(b):
            prepare(b)

        copy.wait()

    for d in range(days):
        spot = int(format(d, "0%db" % stages)[::-1], 2)
        smooth[:, d, :] = gath[spot, 0]
        expo[:, d, :] = gath[spot, 1]
        resid[:, d, :] = gath[spot, 2]

    def each(body):
        @pl.loop(0, group // UNROLL)
        def _(step):
            for i in range(UNROLL):
                body(step * UNROLL + i)

    rows = lax.broadcasted_iota(jnp.int32, (days, BLOCK), 0)
    first_day, last_day = rows == 0, rows == days - 1
    degree = 2.0 - jnp.where(first_day, 1.0, 0.0) - jnp.where(last_day, 1.0, 0.0)

    def prior(slot):
        field_recv = (field_first, field_later)[slot]
        field = pltpu.make_async_remote_copy(
            src_ref=smooth,
            dst_ref=field_recv,
            send_sem=fs_sem.at[slot],
            recv_sem=fr_sem.at[slot],
            device_id=(day, lax.rem(me + last, spaces)),
            device_id_type=MESH,
        )
        back = pltpu.make_async_remote_copy(
            src_ref=back_send,
            dst_ref=back_recv.at[slot],
            send_sem=bs_sem.at[slot],
            recv_sem=br_sem.at[slot],
            device_id=(day, lax.rem(me + 1, spaces)),
            device_id_type=MESH,
        )

        @pl.when(me > 0)
        def _():
            field.start()

        @pl.when(me == last)
        def _():
            field_recv[...] = smooth[...]

        def own(b):
            value = smooth[b]
            both = product(value, w_du[b])
            before = jnp.where(first_day, 0.0, pltpu.roll(value, 1, 0))
            after = jnp.where(last_day, 0.0, pltpu.roll(value, days - 1, 0))
            image[b] = both[:, :BLOCK] + rate_ref[b] * (degree * value - before - after)
            back_tmp[b] = both[:, BLOCK:]

        each(own)

        def permute(b):
            back_send[b] = back_tmp[inverse_ref[b]]

        each(permute)

        @pl.when(me < last)
        def _():
            back.start()
            field.wait_recv()

        def ahead(b):
            image[b] += product(field_recv[column_ref[b]], w_ut[b])

        each(ahead)

        @pl.when(me > 0)
        def _():
            back.wait_recv()
            image[...] += back_recv[slot]
            field.wait_send()

        @pl.when(me == last)
        def _():
            image[...] += back_send[...]

        @pl.when(me < last)
        def _():
            back.wait_send()

    prior(0)
    lat[...] = smooth[...]
    weight[...] = jnp.exp(expo[...])
    resid[...] = resid[...] - weight[...] - image[...]

    def reduced(slot, parts):
        red[slot, me] = jnp.concatenate(
            parts + [jnp.zeros((8 - len(parts), BLOCK), jnp.float32)], axis=0
        )
        copies = []
        for offset in range(1, spaces):
            mine = red.at[slot, me]
            copies.append(
                pltpu.make_async_remote_copy(
                    src_ref=mine,
                    dst_ref=mine,
                    send_sem=rs_sem.at[slot, offset],
                    recv_sem=rr_sem.at[slot, offset],
                    device_id=(day, lax.rem(me + offset, spaces)),
                    device_id_type=MESH,
                )
            )
        for copy in copies:
            copy.start()
        for copy in copies:
            copy.wait()
        total = red[slot, 0]
        for other in range(1, spaces):
            total = total + red[slot, other]
        sums = jnp.sum(total, axis=1, keepdims=True)
        return [sums[i : i + 1] for i in range(len(parts))]

    def across(value):
        return jnp.sum(jnp.sum(value, axis=0), axis=0, keepdims=True)

    one = jnp.ones((1, 1), jnp.float32)

    @pl.loop(0, NEWTON)
    def _(newton):
        direc[...] = jnp.zeros_like(direc)
        dimage[...] = jnp.zeros_like(dimage)
        update[...] = jnp.zeros_like(update)

        def iterate(inner, carry):
            rz_old, curve_old = carry
            count = newton * ITERS + inner

            def precondition(b):
                smooth[b] = product(resid[b], w_m[b])

            each(precondition)
            prior(1)
            image[...] += weight[...] * smooth[...]
            rz, straight, cross = reduced(
                lax.rem(count, 2),
                [
                    across(resid[...] * smooth[...]),
                    across(smooth[...] * image[...]),
                    across(smooth[...] * dimage[...]),
                ],
            )
            ratio = jnp.where(inner == 0, 0.0, rz / rz_old)
            curve = straight + 2.0 * ratio * cross + ratio * ratio * curve_old
            size = rz / curve
            direc[...] = smooth[...] + ratio * direc[...]
            dimage[...] = image[...] + ratio * dimage[...]
            update[...] += size * direc[...]
            resid[...] -= size * dimage[...]
            return rz, curve

        lax.fori_loop(0, ITERS, iterate, (one, one))
        lat[...] += update[...]
        expo[...] += update[...]
        fresh = jnp.exp(expo[...])
        resid[...] = resid[...] + weight[...] * (1.0 + update[...]) - fresh
        weight[...] = fresh

    mine = lax.broadcasted_iota(jnp.int32, (group, days, BLOCK), 1) == day
    latent_out[...] = jnp.sum(jnp.where(mine, lat[...], 0.0), axis=1)
    gradient_out[...] = -jnp.sum(jnp.where(mine, resid[...], 0.0), axis=1)


def on_device(
    latent_start,
    counts,
    log_exposure,
    time_rate,
    diag_blocks,
    upper_blocks,
    columns,
    inverse_panels,
):
    local_days, width = latent_start.shape
    group = diag_blocks.shape[0]
    spaces = lax.axis_size("space")
    days = local_days * lax.axis_size("day")
    stages = days.bit_length() - 1
    target = jnp.minimum(lax.axis_index("space") + 1, spaces - 1)
    local = columns - target * group
    match = local[:, None] == jnp.arange(group)[None, :]
    inverse = jnp.sum(jnp.where(match, jnp.arange(group)[:, None], 0), axis=0).astype(jnp.int32)
    field = (group, days, BLOCK)
    vmem = pl.BlockSpec(memory_space=pltpu.VMEM)
    hbm = pl.BlockSpec(memory_space=pl.ANY)
    smem = pl.BlockSpec(memory_space=pltpu.SMEM)
    sem = pltpu.SemaphoreType.DMA
    f32, bf16 = jnp.float32, jnp.bfloat16
    shape = (group, BLOCK)
    latent, gradient = pl.pallas_call(
        functools.partial(kernel, days, spaces, group),
        out_shape=[jax.ShapeDtypeStruct(shape, f32)] * 2,
        in_specs=[hbm] * 6 + [smem] * 2 + [hbm],
        out_specs=[vmem] * 2,
        scratch_shapes=[
            pltpu.VMEM(shape, f32),
            pltpu.VMEM(shape, jnp.int32),
            pltpu.VMEM(shape, f32),
            pltpu.VMEM((group, 1, BLOCK), f32),
        ]
        + [pltpu.VMEM((group, BLOCK, BLOCK), f32)] * 3
        + [sem((7,))]
        + [pltpu.VMEM((days, 3) + shape, f32)]
        + [pltpu.VMEM(field, f32)] * 13
        + [pltpu.VMEM((2,) + field, f32)]
        + [
            pltpu.VMEM((2, spaces, 8, BLOCK), f32),
            pltpu.VMEM((group, 2 * BLOCK, 2 * BLOCK), bf16),
            pltpu.VMEM((group, 2 * BLOCK, BLOCK), bf16),
            pltpu.VMEM((group, 2 * BLOCK, BLOCK), bf16),
            sem((stages,)),
            sem((stages,)),
            sem((2,)),
            sem((2,)),
            sem((2,)),
            sem((2,)),
            sem((2, spaces)),
            sem((2, spaces)),
        ],
        compiler_params=pltpu.CompilerParams(
            collective_id=0, has_side_effects=True, vmem_limit_bytes=60 * 1024 * 1024
        ),
    )(
        latent_start.reshape(shape),
        counts.reshape(shape),
        log_exposure.reshape(shape),
        time_rate.reshape(group, 1, BLOCK),
        diag_blocks,
        upper_blocks,
        local,
        inverse,
        inverse_panels,
    )
    return latent.reshape(1, width), gradient.reshape(1, width)


def solution(mesh):
    placed = (
        P("day", "space"),
        P("day", "space"),
        P("day", "space"),
        P("space"),
        P("space", None, None),
        P("space", None, None),
        P("space"),
        P("space", None, None),
    )
    return jax.shard_map(
        on_device,
        mesh=mesh,
        in_specs=placed,
        out_specs=(P("day", "space"), P("day", "space")),
        check_vma=False,
    )
```

```python
import functools

import jax
import jax.numpy as jnp
from jax import lax
from jax.experimental import pallas as pl
from jax.experimental.pallas import tpu as pltpu
from jax.sharding import PartitionSpec as P

BLOCK = 128
NEWTON = 2
ITERS = 3
UNROLL = 4
MESH = pl.DeviceIdType.MESH


def orders(days):
    steps = [days >> (stage + 1) for stage in range(days.bit_length() - 1)]
    return steps, steps[:-2] + steps[:-3:-1]


def split(value):
    high = value.astype(jnp.bfloat16)
    low = (value - high.astype(jnp.float32)).astype(jnp.bfloat16)
    return high, low


def product(value, weights):
    rows = value.shape[0]
    high, low = split(value)
    left = jnp.concatenate(
        [jnp.concatenate([high, high], axis=1), jnp.concatenate([low, low], axis=1)], axis=0
    )
    out = jnp.dot(left, weights, preferred_element_type=jnp.float32)
    return out[:rows] + out[rows:]


def kernel(
    days,
    spaces,
    group,
    latent_hbm,
    counts_hbm,
    exposure_hbm,
    rate_hbm,
    diag_hbm,
    upper_hbm,
    column_ref,
    inverse_ref,
    panel_hbm,
    latent_out,
    gradient_out,
    latent_ref,
    counts_ref,
    exposure_ref,
    rate_ref,
    diag_ref,
    upper_ref,
    panel_ref,
    in_sem,
    gath_a,
    gath_b,
    lat,
    expo,
    weight,
    resid,
    smooth,
    direc,
    image,
    dimage,
    update,
    back_tmp,
    back_send,
    field_first,
    field_later,
    back_recv,
    red,
    w_du,
    w_ut,
    w_m,
    gs_sem,
    gr_sem,
    fs_sem,
    fr_sem,
    bs_sem,
    br_sem,
    rs_sem,
    rr_sem,
):
    day = lax.axis_index("day")
    me = lax.axis_index("space")
    last = spaces - 1
    stages = days.bit_length() - 1
    cut = group * 2 // 3
    ways = orders(days)

    def partner(step):
        return day + step - 2 * step * ((day // step) % 2)

    def place_of(index, steps):
        return sum(((index // step) % 2) << stage for stage, step in enumerate(steps))

    sources = (latent_hbm, exposure_hbm, counts_hbm, rate_hbm, diag_hbm, upper_hbm, panel_hbm)
    targets = (latent_ref, exposure_ref, counts_ref, rate_ref, diag_ref, upper_ref, panel_ref)
    loads = [
        pltpu.make_async_copy(source, target, in_sem.at[i])
        for i, (source, target) in enumerate(zip(sources, targets))
    ]
    for load in loads:
        load.start()

    barrier = pltpu.get_barrier_semaphore()
    for step in ways[0]:
        pl.semaphore_signal(barrier, inc=1, device_id=(partner(step), me), device_id_type=MESH)
    for offset in range(1, spaces):
        pl.semaphore_signal(
            barrier, inc=1, device_id=(day, lax.rem(me + offset, spaces)), device_id_type=MESH
        )

    places = [place_of(day, steps) for steps in ways]
    for load in loads[:3]:
        load.wait()
    start = latent_ref[...] + exposure_ref[...]
    gath_a[places[0], :group] = latent_ref[...]
    gath_a[places[0], group:] = start[:cut]
    gath_b[places[1], : group - cut] = start[cut:]
    gath_b[places[1], group - cut :] = counts_ref[...].astype(jnp.float32)

    pl.semaphore_wait(barrier, stages + spaces - 1)

    def prepare(b):
        high, low = split(diag_ref[b])
        w_du[b, :BLOCK, :BLOCK] = high
        w_du[b, BLOCK:, :BLOCK] = low
        upper = upper_ref[b]
        high, low = split(upper)
        w_du[b, :BLOCK, BLOCK:] = high
        w_du[b, BLOCK:, BLOCK:] = low
        high, low = split(upper.T)
        w_ut[b, :BLOCK] = high
        w_ut[b, BLOCK:] = low
        high, low = split(panel_ref[b])
        w_m[b, :BLOCK] = high
        w_m[b, BLOCK:] = low

    def share(way, stage):
        rows = 1 << stage
        base = (places[way] // rows) * rows
        held = (gath_a, gath_b)[way].at[pl.ds(base, rows)]
        return pltpu.make_async_remote_copy(
            src_ref=held,
            dst_ref=held,
            send_sem=gs_sem.at[way, stage],
            recv_sem=gr_sem.at[way, stage],
            device_id=(partner(ways[way][stage]), me),
            device_id_type=MESH,
        )

    def unpack(way, spots):
        for d in range(days):
            spot = place_of(d, ways[way])
            if spot in spots:
                if way == 0:
                    smooth[:, d, :] = gath_a[spot, :group]
                    expo[:cut, d, :] = gath_a[spot, group:]
                else:
                    expo[cut:, d, :] = gath_b[spot, : group - cut]
                    resid[:, d, :] = gath_b[spot, group - cut :]

    for way in range(2):
        share(way, 0).start()
    for load in loads[3:]:
        load.wait()
    for stage in range(stages):
        low, high = group * stage // stages, group * (stage + 1) // stages

        @pl.loop(low, high)
        def _(b):
            prepare(b)

        for way in range(2):
            share(way, stage).wait()
            if stage + 1 < stages:
                share(way, stage + 1).start()
    for way in range(2):
        unpack(way, range(days))

    def each(body):
        @pl.loop(0, group // UNROLL)
        def _(step):
            for i in range(UNROLL):
                body(step * UNROLL + i)

    rows = lax.broadcasted_iota(jnp.int32, (days, BLOCK), 0)
    first_day, last_day = rows == 0, rows == days - 1
    degree = 2.0 - jnp.where(first_day, 1.0, 0.0) - jnp.where(last_day, 1.0, 0.0)

    def prior(slot):
        field_recv = (field_first, field_later)[slot]
        field = pltpu.make_async_remote_copy(
            src_ref=smooth,
            dst_ref=field_recv,
            send_sem=fs_sem.at[slot],
            recv_sem=fr_sem.at[slot],
            device_id=(day, lax.rem(me + last, spaces)),
            device_id_type=MESH,
        )
        back = pltpu.make_async_remote_copy(
            src_ref=back_send,
            dst_ref=back_recv.at[slot],
            send_sem=bs_sem.at[slot],
            recv_sem=br_sem.at[slot],
            device_id=(day, lax.rem(me + 1, spaces)),
            device_id_type=MESH,
        )

        @pl.when(me > 0)
        def _():
            field.start()

        @pl.when(me == last)
        def _():
            field_recv[...] = smooth[...]

        def own(b):
            value = smooth[b]
            both = product(value, w_du[b])
            before = jnp.where(first_day, 0.0, pltpu.roll(value, 1, 0))
            after = jnp.where(last_day, 0.0, pltpu.roll(value, days - 1, 0))
            image[b] = both[:, :BLOCK] + rate_ref[b] * (degree * value - before - after)
            back_tmp[b] = both[:, BLOCK:]

        each(own)

        def permute(b):
            back_send[b] = back_tmp[inverse_ref[b]]

        each(permute)

        @pl.when(me < last)
        def _():
            back.start()
            field.wait_recv()

        def ahead(b):
            image[b] += product(field_recv[column_ref[b]], w_ut[b])

        each(ahead)

        @pl.when(me > 0)
        def _():
            back.wait_recv()
            image[...] += back_recv[slot]
            field.wait_send()

        @pl.when(me == last)
        def _():
            image[...] += back_send[...]

        @pl.when(me < last)
        def _():
            back.wait_send()

    prior(0)
    lat[...] = smooth[...]
    weight[...] = jnp.exp(expo[...])
    resid[...] = resid[...] - weight[...] - image[...]

    def reduced(slot, parts):
        red[slot, me] = jnp.concatenate(
            parts + [jnp.zeros((8 - len(parts), BLOCK), jnp.float32)], axis=0
        )
        copies = []
        for offset in range(1, spaces):
            mine = red.at[slot, me]
            copies.append(
                pltpu.make_async_remote_copy(
                    src_ref=mine,
                    dst_ref=mine,
                    send_sem=rs_sem.at[slot, offset],
                    recv_sem=rr_sem.at[slot, offset],
                    device_id=(day, lax.rem(me + offset, spaces)),
                    device_id_type=MESH,
                )
            )
        for copy in copies:
            copy.start()
        for copy in copies:
            copy.wait()
        total = red[slot, 0]
        for other in range(1, spaces):
            total = total + red[slot, other]
        sums = jnp.sum(total, axis=1, keepdims=True)
        return [sums[i : i + 1] for i in range(len(parts))]

    def across(value):
        return jnp.sum(jnp.sum(value, axis=0), axis=0, keepdims=True)

    one = jnp.ones((1, 1), jnp.float32)

    @pl.loop(0, NEWTON)
    def _(newton):
        direc[...] = jnp.zeros_like(direc)
        dimage[...] = jnp.zeros_like(dimage)
        update[...] = jnp.zeros_like(update)

        def iterate(inner, carry):
            rz_old, curve_old = carry
            count = newton * ITERS + inner

            def precondition(b):
                smooth[b] = product(resid[b], w_m[b])

            each(precondition)
            prior(1)
            image[...] += weight[...] * smooth[...]
            rz, straight, cross = reduced(
                lax.rem(count, 2),
                [
                    across(resid[...] * smooth[...]),
                    across(smooth[...] * image[...]),
                    across(smooth[...] * dimage[...]),
                ],
            )
            ratio = jnp.where(inner == 0, 0.0, rz / rz_old)
            curve = straight + 2.0 * ratio * cross + ratio * ratio * curve_old
            size = rz / curve
            direc[...] = smooth[...] + ratio * direc[...]
            dimage[...] = image[...] + ratio * dimage[...]
            update[...] += size * direc[...]
            resid[...] -= size * dimage[...]
            return rz, curve

        lax.fori_loop(0, ITERS, iterate, (one, one))
        lat[...] += update[...]
        expo[...] += update[...]
        fresh = jnp.exp(expo[...])
        resid[...] = resid[...] + weight[...] * (1.0 + update[...]) - fresh
        weight[...] = fresh

    mine = lax.broadcasted_iota(jnp.int32, (group, days, BLOCK), 1) == day
    latent_out[...] = jnp.sum(jnp.where(mine, lat[...], 0.0), axis=1)
    gradient_out[...] = -jnp.sum(jnp.where(mine, resid[...], 0.0), axis=1)


def on_device(
    latent_start,
    counts,
    log_exposure,
    time_rate,
    diag_blocks,
    upper_blocks,
    columns,
    inverse_panels,
):
    local_days, width = latent_start.shape
    group = diag_blocks.shape[0]
    spaces = lax.axis_size("space")
    days = local_days * lax.axis_size("day")
    stages = days.bit_length() - 1
    target = jnp.minimum(lax.axis_index("space") + 1, spaces - 1)
    local = columns - target * group
    match = local[:, None] == jnp.arange(group)[None, :]
    inverse = jnp.sum(jnp.where(match, jnp.arange(group)[:, None], 0), axis=0).astype(jnp.int32)
    field = (group, days, BLOCK)
    vmem = pl.BlockSpec(memory_space=pltpu.VMEM)
    hbm = pl.BlockSpec(memory_space=pl.ANY)
    smem = pl.BlockSpec(memory_space=pltpu.SMEM)
    sem = pltpu.SemaphoreType.DMA
    f32, bf16 = jnp.float32, jnp.bfloat16
    shape = (group, BLOCK)
    latent, gradient = pl.pallas_call(
        functools.partial(kernel, days, spaces, group),
        out_shape=[jax.ShapeDtypeStruct(shape, f32)] * 2,
        in_specs=[hbm] * 6 + [smem] * 2 + [hbm],
        out_specs=[vmem] * 2,
        scratch_shapes=[
            pltpu.VMEM(shape, f32),
            pltpu.VMEM(shape, jnp.int32),
            pltpu.VMEM(shape, f32),
            pltpu.VMEM((group, 1, BLOCK), f32),
        ]
        + [pltpu.VMEM((group, BLOCK, BLOCK), f32)] * 3
        + [sem((7,))]
        + [
            pltpu.VMEM((days, group + group * 2 // 3, BLOCK), f32),
            pltpu.VMEM((days, 2 * group - group * 2 // 3, BLOCK), f32),
        ]
        + [pltpu.VMEM(field, f32)] * 13
        + [pltpu.VMEM((2,) + field, f32)]
        + [
            pltpu.VMEM((2, spaces, 8, BLOCK), f32),
            pltpu.VMEM((group, 2 * BLOCK, 2 * BLOCK), bf16),
            pltpu.VMEM((group, 2 * BLOCK, BLOCK), bf16),
            pltpu.VMEM((group, 2 * BLOCK, BLOCK), bf16),
            sem((2, stages)),
            sem((2, stages)),
            sem((2,)),
            sem((2,)),
            sem((2,)),
            sem((2,)),
            sem((2, spaces)),
            sem((2, spaces)),
        ],
        compiler_params=pltpu.CompilerParams(
            collective_id=0, has_side_effects=True, vmem_limit_bytes=60 * 1024 * 1024
        ),
    )(
        latent_start.reshape(shape),
        counts.reshape(shape),
        log_exposure.reshape(shape),
        time_rate.reshape(group, 1, BLOCK),
        diag_blocks,
        upper_blocks,
        local,
        inverse,
        inverse_panels,
    )
    return latent.reshape(1, width), gradient.reshape(1, width)


def solution(mesh):
    placed = (
        P("day", "space"),
        P("day", "space"),
        P("day", "space"),
        P("space"),
        P("space", None, None),
        P("space", None, None),
        P("space"),
        P("space", None, None),
    )
    return jax.shard_map(
        on_device,
        mesh=mesh,
        in_specs=placed,
        out_specs=(P("day", "space"), P("day", "space")),
        check_vma=False,
    )
```

```python
import functools

import jax
import jax.numpy as jnp
from jax import lax
from jax.experimental import pallas as pl
from jax.experimental.pallas import tpu as pltpu
from jax.sharding import PartitionSpec as P

BLOCK = 128
NEWTON = 2
ITERS = 3
UNROLL = 24
MESH = pl.DeviceIdType.MESH


def orders(days):
    steps = [days >> (stage + 1) for stage in range(days.bit_length() - 1)]
    return steps, steps[:-2] + steps[:-3:-1]


def split(value):
    high = value.astype(jnp.bfloat16)
    low = (value - high.astype(jnp.float32)).astype(jnp.bfloat16)
    return high, low


def product(value, weights):
    rows = value.shape[0]
    high, low = split(value)
    left = jnp.concatenate(
        [jnp.concatenate([high, high], axis=1), jnp.concatenate([low, low], axis=1)], axis=0
    )
    out = jnp.dot(left, weights, preferred_element_type=jnp.float32)
    return out[:rows] + out[rows:]


def kernel(
    days,
    spaces,
    group,
    latent_hbm,
    counts_hbm,
    exposure_hbm,
    rate_hbm,
    diag_hbm,
    upper_hbm,
    column_ref,
    inverse_ref,
    panel_hbm,
    latent_out,
    gradient_out,
    latent_ref,
    counts_ref,
    exposure_ref,
    rate_ref,
    diag_ref,
    upper_ref,
    panel_ref,
    in_sem,
    gath_a,
    gath_b,
    lat,
    expo,
    weight,
    resid,
    smooth,
    direc,
    image,
    dimage,
    update,
    back_tmp,
    back_send,
    field_first,
    field_later,
    back_recv,
    red,
    w_du,
    w_ut,
    w_m,
    gs_sem,
    gr_sem,
    fs_sem,
    fr_sem,
    bs_sem,
    br_sem,
    rs_sem,
    rr_sem,
):
    day = lax.axis_index("day")
    me = lax.axis_index("space")
    last = spaces - 1
    stages = days.bit_length() - 1
    cut = group * 2 // 3
    ways = orders(days)

    def partner(step):
        return day + step - 2 * step * ((day // step) % 2)

    def place_of(index, steps):
        return sum(((index // step) % 2) << stage for stage, step in enumerate(steps))

    sources = (latent_hbm, exposure_hbm, counts_hbm, rate_hbm, diag_hbm, upper_hbm, panel_hbm)
    targets = (latent_ref, exposure_ref, counts_ref, rate_ref, diag_ref, upper_ref, panel_ref)
    loads = [
        pltpu.make_async_copy(source, target, in_sem.at[i])
        for i, (source, target) in enumerate(zip(sources, targets))
    ]
    for load in loads:
        load.start()

    barrier = pltpu.get_barrier_semaphore()
    for step in ways[0]:
        pl.semaphore_signal(barrier, inc=1, device_id=(partner(step), me), device_id_type=MESH)
    for offset in range(1, spaces):
        pl.semaphore_signal(
            barrier, inc=1, device_id=(day, lax.rem(me + offset, spaces)), device_id_type=MESH
        )

    places = [place_of(day, steps) for steps in ways]
    for load in loads[:3]:
        load.wait()
    start = latent_ref[...] + exposure_ref[...]
    gath_a[places[0], :group] = latent_ref[...]
    gath_a[places[0], group:] = start[:cut]
    gath_b[places[1], : group - cut] = start[cut:]
    gath_b[places[1], group - cut :] = counts_ref[...].astype(jnp.float32)

    pl.semaphore_wait(barrier, stages + spaces - 1)

    def prepare(b):
        high, low = split(diag_ref[b])
        w_du[b, :BLOCK, :BLOCK] = high
        w_du[b, BLOCK:, :BLOCK] = low
        upper = upper_ref[b]
        high, low = split(upper)
        w_du[b, :BLOCK, BLOCK:] = high
        w_du[b, BLOCK:, BLOCK:] = low
        high, low = split(upper.T)
        w_ut[b, :BLOCK] = high
        w_ut[b, BLOCK:] = low
        high, low = split(panel_ref[b])
        w_m[b, :BLOCK] = high
        w_m[b, BLOCK:] = low

    def share(way, stage):
        rows = 1 << stage
        base = (places[way] // rows) * rows
        held = (gath_a, gath_b)[way].at[pl.ds(base, rows)]
        return pltpu.make_async_remote_copy(
            src_ref=held,
            dst_ref=held,
            send_sem=gs_sem.at[way, stage],
            recv_sem=gr_sem.at[way, stage],
            device_id=(partner(ways[way][stage]), me),
            device_id_type=MESH,
        )

    def unpack(way, spots):
        for d in range(days):
            spot = place_of(d, ways[way])
            if spot in spots:
                if way == 0:
                    smooth[:, d, :] = gath_a[spot, :group]
                    expo[:cut, d, :] = gath_a[spot, group:]
                else:
                    expo[cut:, d, :] = gath_b[spot, : group - cut]
                    resid[:, d, :] = gath_b[spot, group - cut :]

    for way in range(2):
        share(way, 0).start()
    for load in loads[3:]:
        load.wait()
    for stage in range(stages):
        low, high = group * stage // stages, group * (stage + 1) // stages

        @pl.loop(low, high)
        def _(b):
            prepare(b)

        for way in range(2):
            share(way, stage).wait()
            if stage + 1 < stages:
                share(way, stage + 1).start()
    for way in range(2):
        unpack(way, range(days))

    def each(body):
        @pl.loop(0, group // UNROLL)
        def _(step):
            blocks = [step * UNROLL + i for i in range(UNROLL)]
            for b, stores in [(b, body(b)) for b in blocks]:
                for ref, value in stores:
                    ref[b] = value

    rows = lax.broadcasted_iota(jnp.int32, (days, BLOCK), 0)
    first_day, last_day = rows == 0, rows == days - 1
    degree = 2.0 - jnp.where(first_day, 1.0, 0.0) - jnp.where(last_day, 1.0, 0.0)

    def prior(slot):
        field_recv = (field_first, field_later)[slot]
        field = pltpu.make_async_remote_copy(
            src_ref=smooth,
            dst_ref=field_recv,
            send_sem=fs_sem.at[slot],
            recv_sem=fr_sem.at[slot],
            device_id=(day, lax.rem(me + last, spaces)),
            device_id_type=MESH,
        )
        back = pltpu.make_async_remote_copy(
            src_ref=back_send,
            dst_ref=back_recv.at[slot],
            send_sem=bs_sem.at[slot],
            recv_sem=br_sem.at[slot],
            device_id=(day, lax.rem(me + 1, spaces)),
            device_id_type=MESH,
        )

        @pl.when(me > 0)
        def _():
            field.start()

        @pl.when(me == last)
        def _():
            field_recv[...] = smooth[...]

        def own(b):
            value = smooth[b]
            both = product(value, w_du[b])
            before = jnp.where(first_day, 0.0, pltpu.roll(value, 1, 0))
            after = jnp.where(last_day, 0.0, pltpu.roll(value, days - 1, 0))
            temporal = rate_ref[b] * (degree * value - before - after)
            return (image, both[:, :BLOCK] + temporal), (back_tmp, both[:, BLOCK:])

        each(own)

        def permute(b):
            return ((back_send, back_tmp[inverse_ref[b]]),)

        each(permute)

        @pl.when(me < last)
        def _():
            back.start()
            field.wait_recv()

        def ahead(b):
            return ((image, image[b] + product(field_recv[column_ref[b]], w_ut[b])),)

        each(ahead)

        @pl.when(me > 0)
        def _():
            back.wait_recv()
            image[...] += back_recv[slot]
            field.wait_send()

        @pl.when(me == last)
        def _():
            image[...] += back_send[...]

        @pl.when(me < last)
        def _():
            back.wait_send()

    prior(0)
    lat[...] = smooth[...]
    weight[...] = jnp.exp(expo[...])
    resid[...] = resid[...] - weight[...] - image[...]

    def reduced(slot, parts):
        red[slot, me] = jnp.concatenate(
            parts + [jnp.zeros((8 - len(parts), BLOCK), jnp.float32)], axis=0
        )
        copies = []
        for offset in range(1, spaces):
            mine = red.at[slot, me]
            copies.append(
                pltpu.make_async_remote_copy(
                    src_ref=mine,
                    dst_ref=mine,
                    send_sem=rs_sem.at[slot, offset],
                    recv_sem=rr_sem.at[slot, offset],
                    device_id=(day, lax.rem(me + offset, spaces)),
                    device_id_type=MESH,
                )
            )
        for copy in copies:
            copy.start()
        for copy in copies:
            copy.wait()
        total = red[slot, 0]
        for other in range(1, spaces):
            total = total + red[slot, other]
        sums = jnp.sum(total, axis=1, keepdims=True)
        return [sums[i : i + 1] for i in range(len(parts))]

    def across(value):
        return jnp.sum(jnp.sum(value, axis=0), axis=0, keepdims=True)

    one = jnp.ones((1, 1), jnp.float32)

    @pl.loop(0, NEWTON)
    def _(newton):
        direc[...] = jnp.zeros_like(direc)
        dimage[...] = jnp.zeros_like(dimage)
        update[...] = jnp.zeros_like(update)

        def iterate(inner, carry):
            rz_old, curve_old = carry
            count = newton * ITERS + inner

            def precondition(b):
                return ((smooth, product(resid[b], w_m[b])),)

            each(precondition)
            prior(1)
            image[...] += weight[...] * smooth[...]
            rz, straight, cross = reduced(
                lax.rem(count, 2),
                [
                    across(resid[...] * smooth[...]),
                    across(smooth[...] * image[...]),
                    across(smooth[...] * dimage[...]),
                ],
            )
            ratio = jnp.where(inner == 0, 0.0, rz / rz_old)
            curve = straight + 2.0 * ratio * cross + ratio * ratio * curve_old
            size = rz / curve
            direc[...] = smooth[...] + ratio * direc[...]
            dimage[...] = image[...] + ratio * dimage[...]
            update[...] += size * direc[...]
            resid[...] -= size * dimage[...]
            return rz, curve

        lax.fori_loop(0, ITERS, iterate, (one, one))
        lat[...] += update[...]
        expo[...] += update[...]
        fresh = jnp.exp(expo[...])
        resid[...] = resid[...] + weight[...] * (1.0 + update[...]) - fresh
        weight[...] = fresh

    mine = lax.broadcasted_iota(jnp.int32, (group, days, BLOCK), 1) == day
    latent_out[...] = jnp.sum(jnp.where(mine, lat[...], 0.0), axis=1)
    gradient_out[...] = -jnp.sum(jnp.where(mine, resid[...], 0.0), axis=1)


def on_device(
    latent_start,
    counts,
    log_exposure,
    time_rate,
    diag_blocks,
    upper_blocks,
    columns,
    inverse_panels,
):
    local_days, width = latent_start.shape
    group = diag_blocks.shape[0]
    spaces = lax.axis_size("space")
    days = local_days * lax.axis_size("day")
    stages = days.bit_length() - 1
    target = jnp.minimum(lax.axis_index("space") + 1, spaces - 1)
    local = columns - target * group
    match = local[:, None] == jnp.arange(group)[None, :]
    inverse = jnp.sum(jnp.where(match, jnp.arange(group)[:, None], 0), axis=0).astype(jnp.int32)
    field = (group, days, BLOCK)
    vmem = pl.BlockSpec(memory_space=pltpu.VMEM)
    hbm = pl.BlockSpec(memory_space=pl.ANY)
    smem = pl.BlockSpec(memory_space=pltpu.SMEM)
    sem = pltpu.SemaphoreType.DMA
    f32, bf16 = jnp.float32, jnp.bfloat16
    shape = (group, BLOCK)
    latent, gradient = pl.pallas_call(
        functools.partial(kernel, days, spaces, group),
        out_shape=[jax.ShapeDtypeStruct(shape, f32)] * 2,
        in_specs=[hbm] * 6 + [smem] * 2 + [hbm],
        out_specs=[vmem] * 2,
        scratch_shapes=[
            pltpu.VMEM(shape, f32),
            pltpu.VMEM(shape, jnp.int32),
            pltpu.VMEM(shape, f32),
            pltpu.VMEM((group, 1, BLOCK), f32),
        ]
        + [pltpu.VMEM((group, BLOCK, BLOCK), f32)] * 3
        + [sem((7,))]
        + [
            pltpu.VMEM((days, group + group * 2 // 3, BLOCK), f32),
            pltpu.VMEM((days, 2 * group - group * 2 // 3, BLOCK), f32),
        ]
        + [pltpu.VMEM(field, f32)] * 13
        + [pltpu.VMEM((2,) + field, f32)]
        + [
            pltpu.VMEM((2, spaces, 8, BLOCK), f32),
            pltpu.VMEM((group, 2 * BLOCK, 2 * BLOCK), bf16),
            pltpu.VMEM((group, 2 * BLOCK, BLOCK), bf16),
            pltpu.VMEM((group, 2 * BLOCK, BLOCK), bf16),
            sem((2, stages)),
            sem((2, stages)),
            sem((2,)),
            sem((2,)),
            sem((2,)),
            sem((2,)),
            sem((2, spaces)),
            sem((2, spaces)),
        ],
        compiler_params=pltpu.CompilerParams(
            collective_id=0, has_side_effects=True, vmem_limit_bytes=60 * 1024 * 1024
        ),
    )(
        latent_start.reshape(shape),
        counts.reshape(shape),
        log_exposure.reshape(shape),
        time_rate.reshape(group, 1, BLOCK),
        diag_blocks,
        upper_blocks,
        local,
        inverse,
        inverse_panels,
    )
    return latent.reshape(1, width), gradient.reshape(1, width)


def solution(mesh):
    placed = (
        P("day", "space"),
        P("day", "space"),
        P("day", "space"),
        P("space"),
        P("space", None, None),
        P("space", None, None),
        P("space"),
        P("space", None, None),
    )
    return jax.shard_map(
        on_device,
        mesh=mesh,
        in_specs=placed,
        out_specs=(P("day", "space"), P("day", "space")),
        check_vma=False,
    )
```
